32 devices in a mesh: grp: 2 (over y), gx: 4 (over z), gy: 4 (over x, core).
Axes of the slice: x: 2, y: 2, z: 4, core: 2. Of those that a mesh axis runs over, the one named last changes fastest.
Arguments:
- velocity: bfloat16 [8, 64, 64, 128], P(('grp', 'gx'), None, 'gy'), parts along dimension 0, may hold values from 0.19921875 to 0.41992188
- log_density: bfloat16 [8, 64, 64, 128], P(('grp', 'gx'), None, 'gy'), parts along dimension 0, may hold values from 0 to 0.69921875
- fwd_prev: bfloat16 [8, 256, 64, 128], P(('grp', 'gx'), None, 'gy'), parts along dimension 0, may hold values from -6 to 6
- fwd_now: bfloat16 [8, 256, 64, 128], P(('grp', 'gx'), None, 'gy'), parts along dimension 0, may hold values from -6 to 6
- adj_now: bfloat16 [8, 256, 64, 128], P(('grp', 'gx'), None, 'gy'), parts along dimension 0, may hold values from -6 to 6
- adj_next: bfloat16 [8, 256, 64, 128], P(('grp', 'gx'), None, 'gy'), parts along dimension 0, may hold values from -6 to 6
- wavelet: float32 [8, 3], P(('grp', 'gx')), parts along dimension 0, may hold values from -16 to 16
- source_pos: int32 [8, 3], P(('grp', 'gx')), parts along dimension 0, may hold values from 0 to 127, as said below
- receiver_pos: int32 [8, 3, 256], P(('grp', 'gx')), parts along dimension 0, may hold values from 0 to 127, as said below
- observed: float32 [8, 3, 256], P(('grp', 'gx')), parts along dimension 0, may hold values from -6 to 6
- footprint: int32 [8, 4], P('grp'), parts along dimension 0, may hold values from -1 to 3, as said below
- owner: int32 [4], replicated, may hold values from 0 to 3, each once
Outputs:
- smoothed: float32 [256, 64, 256], P(('grp', 'gx'), 'gy'), parts along dimension 0
The draws below stay inside these ranges and needn't reach their ends.
There are 2 independent parts, one for each index of `grp`. The reference program is written for one: setup_inputs(seed, part) draws one part's arguments, and reference() takes and returns one part's arrays. A program takes and returns all parts, laid end to end along the dimension named above; an argument that names none is the same for every part. Nothing has to cross between parts.
Inputs may be any that keep to these rules, and one draw needn't show every extreme that they name: `footprint`: each row lists blocks start, start + 1, ... in its first two or more slots and -1 after them; some row starts at block 0 and some row ends at block 3, both with all 4 slots live. `source_pos`: source cells lie in the first 128 cells of the window along the first dimension, within the window along the others; some shot's source is at the last such cell in every component and some other shot's at cell 0 in every component. `receiver_pos`: receiver cells lie in the first 128 cells of the window along the first dimension, within the window along the others; some receiver is at the last such cell in every component and some other at cell 0 in every component. `owner`: each index of gx holds exactly one block.
All inputs are finite; a program needn't handle non-finite values.
Results may differ from the reference program's by a relative error of at most 0.0003.
Values may be sent and summed in bfloat16 or wider, within the bound.
A program may use at most 128 MiB of HBM per device.

```python
import math
import jax
import jax.numpy as jnp
from jax import lax

CX = 64
NZ = 128
FPB = 4
NT = 3
NREC = 256
W = 256
NBLK = 4
SHOTS = 4
NX = 256
NY = 64


def draw_footprint(key, part):
    key = jax.random.fold_in(key, 11)
    keys = jax.random.split(key, 4)
    starts = jax.random.randint(keys[0], (SHOTS,), 0, NBLK - FPB + 1)
    counts = jax.random.randint(keys[1], (SHOTS,), 2, FPB + 1)
    first_row = jax.random.randint(keys[2], (), 0, SHOTS)
    second_row = (first_row + 1 + jax.random.randint(keys[3], (), 0, SHOTS - 1)) % SHOTS
    rows = jnp.arange(SHOTS)
    starts = jnp.where(rows == first_row, 0, starts)
    starts = jnp.where(rows == second_row, NBLK - FPB, starts)
    counts = jnp.where((rows == first_row) | (rows == second_row), FPB, counts)
    slots = jnp.arange(FPB)
    listed = jnp.where(slots[None, :] < counts[:, None], starts[:, None] + slots[None, :], -1)
    return listed.astype(jnp.int32)


def draw_source_pos(key, part):
    key = jax.random.fold_in(key, 12)
    keys = jax.random.split(key, 5)
    first = jax.random.randint(keys[0], (SHOTS,), 0, 2 * CX)
    second = jax.random.randint(keys[1], (SHOTS,), 0, NY)
    third = jax.random.randint(keys[2], (SHOTS,), 0, NZ)
    upper_row = jax.random.randint(keys[3], (), 0, SHOTS)
    lower_row = (upper_row + 1 + jax.random.randint(keys[4], (), 0, SHOTS - 1)) % SHOTS
    rows = jnp.arange(SHOTS)
    first = jnp.where(rows == upper_row, 2 * CX - 1, jnp.where(rows == lower_row, 0, first))
    second = jnp.where(rows == upper_row, NY - 1, jnp.where(rows == lower_row, 0, second))
    third = jnp.where(rows == upper_row, NZ - 1, jnp.where(rows == lower_row, 0, third))
    return jnp.stack([first, second, third], axis=1).astype(jnp.int32)


def draw_receiver_pos(key, part):
    key = jax.random.fold_in(key, 13)
    keys = jax.random.split(key, 6)
    first = jax.random.randint(keys[0], (SHOTS, NREC), 0, 2 * CX)
    second = jax.random.randint(keys[1], (SHOTS, NREC), 0, NY)
    third = jax.random.randint(keys[2], (SHOTS, NREC), 0, NZ)
    chosen_shot = jax.random.randint(keys[3], (), 0, SHOTS)
    upper_slot = jax.random.randint(keys[4], (), 0, NREC)
    lower_slot = (upper_slot + 1 + jax.random.randint(keys[5], (), 0, NREC - 1)) % NREC
    rows = jnp.arange(SHOTS)[:, None]
    slots = jnp.arange(NREC)[None, :]
    upper = (rows == chosen_shot) & (slots == upper_slot)
    lower = (rows == chosen_shot) & (slots == lower_slot)
    first = jnp.where(upper, 2 * CX - 1, jnp.where(lower, 0, first))
    second = jnp.where(upper, NY - 1, jnp.where(lower, 0, second))
    third = jnp.where(upper, NZ - 1, jnp.where(lower, 0, third))
    return jnp.stack([first, second, third], axis=1).astype(jnp.int32)


def level_of(rng, shape, cuts, smallest, largest):
    gain = 1.0
    for position, blocks in cuts:
        heights = jax.random.uniform(jax.random.fold_in(jax.random.fold_in(rng, 6), position), (blocks,), jnp.float32, smallest / len(cuts), largest / len(cuts))
        gain = gain * jnp.repeat(jnp.exp(heights), shape[position] // blocks).reshape((-1,) + (1,) * (len(shape) - 1 - position))
    return gain


def bell_draw(key, dims, width, limit, shards=(), kind=jnp.bfloat16):
    drawn = width * jax.random.normal(key, dims, jnp.float32)
    if shards:
        drawn = drawn * level_of(key, dims, shards, -0.22, 0.18)
    return jnp.clip(drawn, -limit, limit).astype(kind)


def setup_inputs(seed: int = 0, part: int = 0) -> dict:
    streams_of = jax.random.split(jax.random.key(seed), 13)
    part_splits = jax.random.split(jax.random.fold_in(streams_of[12], part), 13)
    velocity = jnp.clip(jnp.exp(math.log(0.41992188) - 0.7456652 * jax.random.uniform(part_splits[0], (NBLK, CX, NY, NZ), jnp.float32) ** level_of(part_splits[0], (NBLK, CX, NY, NZ), ((0, 4), (2, 4)), -0.2, 0.2)), 0.19921875, 0.41992188).astype(jnp.bfloat16)
    log_density = jnp.clip(0.69921875 * jax.random.uniform(part_splits[1], (NBLK, CX, NY, NZ), jnp.float32) ** level_of(part_splits[1], (NBLK, CX, NY, NZ), ((0, 4), (2, 4)), -0.2, 0.2), 0.0, 0.69921875).astype(jnp.bfloat16)
    fwd_prev = bell_draw(part_splits[2], (SHOTS, W, NY, NZ), 1.0, 6.0, ((0, 4), (2, 4)))
    fwd_now = bell_draw(part_splits[3], (SHOTS, W, NY, NZ), 1.0, 6.0, ((0, 4), (2, 4)))
    adj_now = bell_draw(part_splits[4], (SHOTS, W, NY, NZ), 1.0, 6.0, ((0, 4), (2, 4)))
    adj_next = bell_draw(part_splits[5], (SHOTS, W, NY, NZ), 1.0, 6.0, ((0, 4), (2, 4)))
    wavelet = bell_draw(part_splits[6], (SHOTS, NT), 4.0, 16.0, ((0, 4),), jnp.float32)
    source_pos = draw_source_pos(jax.random.fold_in(jax.random.fold_in(streams_of[12], part), 71), part)
    receiver_pos = draw_receiver_pos(jax.random.fold_in(jax.random.fold_in(streams_of[12], part), 71), part)
    observed = bell_draw(part_splits[9], (SHOTS, NT, NREC), 1.0, 6.0, ((0, 4),), jnp.float32)
    footprint = draw_footprint(jax.random.fold_in(jax.random.fold_in(streams_of[12], part), 71), part)
    owner = jax.random.permutation(streams_of[11], NBLK).astype(jnp.int32)
    return {"velocity": velocity, "log_density": log_density, "fwd_prev": fwd_prev, "fwd_now": fwd_now, "adj_now": adj_now, "adj_next": adj_next, "wavelet": wavelet, "source_pos": source_pos, "receiver_pos": receiver_pos, "observed": observed, "footprint": footprint, "owner": owner}


SECOND = (-205.0 / 72.0, 8.0 / 5.0, -1.0 / 5.0, 8.0 / 315.0, -1.0 / 560.0)
FIRST = (4.0 / 5.0, -1.0 / 5.0, 4.0 / 105.0, -1.0 / 280.0)


def derivatives(padded, extent):
    def shifted(dimension, offset):
        starts = [4, 4, 4]
        starts[dimension] = 4 + offset
        return padded[starts[0]:starts[0] + extent[0], starts[1]:starts[1] + extent[1], starts[2]:starts[2] + extent[2]]

    laplace = (3.0 * SECOND[0]) * shifted(0, 0)
    slopes = []
    for dimension in range(3):
        slope_sum = jnp.zeros(extent, jnp.float32)
        for offset in range(1, 5):
            ahead_cells = shifted(dimension, offset)
            behind = shifted(dimension, -offset)
            laplace = laplace + SECOND[offset] * (ahead_cells + behind)
            slope_sum = slope_sum + FIRST[offset - 1] * (ahead_cells - behind)
        slopes.append(slope_sum)
    return laplace, slopes


def operator(padded, extent, squared, density_slopes):
    laplace, slopes = derivatives(padded, extent)
    advect = density_slopes[0] * slopes[0] + density_slopes[1] * slopes[1] + density_slopes[2] * slopes[2]
    return squared * (laplace - advect)


def kernels(depth_values, cells):
    positions = jnp.arange(cells, dtype=jnp.float32)
    distance = jnp.abs(positions[:, None] - positions[None, :])
    lengths = CX * (1.5 + 4.5 * depth_values / (NZ - 1.0))
    weights = jnp.exp(-distance[None, :, :] / lengths[:, None, None])
    return weights / jnp.sum(weights, axis=2, keepdims=True)


def reference(velocity, log_density, fwd_prev, fwd_now, adj_now, adj_next, wavelet, source_pos, receiver_pos, observed, footprint, owner):
    speed_x = velocity[owner]
    density_x = log_density[owner]
    extent = (FPB * CX, NY, NZ)
    x_cells = jnp.arange(FPB * CX)[:, None, None]
    y_cells = jnp.arange(NY)[None, :, None]
    z_cells = jnp.arange(NZ)[None, None, :]

    def one_shot(gradient, shot):
        blocks = footprint[shot]
        live = blocks >= 0
        safe = jnp.maximum(blocks, 0)
        livef = live.astype(jnp.float32)[:, None, None, None]
        speed = speed_x[safe].astype(jnp.float32)
        squared = (speed * speed * livef).reshape(extent)
        mask = jnp.broadcast_to(livef, speed.shape).reshape(extent)
        density = (density_x[safe].astype(jnp.float32) * livef).reshape(extent)
        unused, density_slopes = derivatives(jnp.pad(density, 4), extent)
        spot = source_pos[shot]
        source = ((x_cells == spot[0]) & (y_cells == spot[1]) & (z_cells == spot[2])).astype(jnp.float32) * mask
        rec_x = receiver_pos[shot, 0]
        rec_y = receiver_pos[shot, 1]
        rec_z = receiver_pos[shot, 2]
        states = [fwd_prev[shot].astype(jnp.float32) * mask, fwd_now[shot].astype(jnp.float32) * mask]
        residuals = []
        for tick in range(NT):
            older = states[-2]
            current = states[-1]
            newer = 2.0 * current - older + operator(jnp.pad(current, 4), extent, squared, density_slopes) + wavelet[shot, tick] * source
            states.append(newer)
            residuals.append(newer[rec_x, rec_y, rec_z] - observed[shot, tick])
        far_state = adj_next[shot].astype(jnp.float32) * mask
        near_state = adj_now[shot].astype(jnp.float32) * mask
        image = jnp.zeros(extent, jnp.float32)
        for tick in reversed(range(NT)):
            inject = jnp.zeros(extent, jnp.float32).at[rec_x, rec_y, rec_z].add(residuals[tick])
            nearer = 2.0 * near_state - far_state + operator(jnp.pad(near_state, 4), extent, squared, density_slopes) + inject * mask
            image = image + nearer * (states[tick + 2] - 2.0 * states[tick + 1] + states[tick])
            far_state = near_state
            near_state = nearer
        pieces = image.reshape(FPB, CX, NY, NZ)
        for slot in range(FPB):
            gradient = gradient.at[safe[slot]].add(pieces[slot] * live[slot].astype(jnp.float32))
        return gradient, None

    gradient, unused = lax.scan(one_shot, jnp.zeros((NBLK, CX, NY, NZ), jnp.float32), jnp.arange(SHOTS))
    field = gradient.reshape(NX, NY, NZ)

    def smooth(depth):
        kernel = kernels(depth.astype(jnp.float32)[None], NX)[0]
        column = lax.dynamic_index_in_dim(field, depth, 2, keepdims=False)
        return jnp.dot(kernel, column, precision=lax.Precision.HIGHEST).T

    return lax.map(smooth, jnp.arange(NZ))
```

```python
import functools

import jax
import jax.numpy as jnp
import numpy as np
from jax import lax
from jax.experimental import pallas as pl
from jax.experimental.pallas import tpu as pltpu
from jax.sharding import PartitionSpec as P

CX = 64
NZ = 128
NT = 3
H = 4
SECOND = (-14350.0, 8064.0, -1008.0, 128.0, -9.0)
FIRST = (672.0, -168.0, 32.0, -3.0)
BF = jnp.bfloat16
F32 = jnp.float32
CHUNK = 32


def band(size):
    first = np.zeros((size, size), np.float32)
    second = np.zeros((size, size), np.float32)
    for k in range(1, 5):
        ahead = np.eye(size, k=k, dtype=np.float32)
        first += FIRST[k - 1] * (ahead - ahead.T)
        second += SECOND[k] * (ahead + ahead.T)
    return first, second


def dot(a, b):
    return jnp.dot(a, b, preferred_element_type=F32)


def split(u):
    hi = u.astype(BF)
    return hi, (u - hi.astype(F32)).astype(BF)


def wave_kernel(
    dims,
    scal, fprev, fnow, anow, anext, speed, dens, maskp, code_col, code_row, recz, obs, dx, mz,
    out,
    p0, p1, p2, q3, q2, q1, acc, sq, grad, den, xt, xo, hot, vsum, inj,
    send_sem, recv_sem,
):
    rows, span, depth = dims
    half = span // 2
    gy = lax.axis_index("gy")
    count = lax.axis_size("gy")
    has_left = gy > 0
    has_right = gy < count - 1
    barrier = pltpu.get_barrier_semaphore()
    steps = (den, p0, q3, p1, p2, q2, q1)

    @pl.when(has_left)
    def _():
        pl.semaphore_signal(barrier, inc=1, device_id={"gy": gy - 1}, device_id_type=pl.DeviceIdType.MESH)

    @pl.when(has_right)
    def _():
        pl.semaphore_signal(barrier, inc=1, device_id={"gy": gy + 1}, device_id_type=pl.DeviceIdType.MESH)

    @pl.when(jnp.logical_not(has_left))
    def _():
        for buf in steps:
            buf[0:H] = jnp.zeros((H, span, depth), buf.dtype)

    @pl.when(jnp.logical_not(has_right))
    def _():
        for buf in steps:
            buf[rows + H : rows + 2 * H] = jnp.zeros((H, span, depth), buf.dtype)

    pl.semaphore_wait(barrier, has_left.astype(jnp.int32) + has_right.astype(jnp.int32))

    def to_left(e):
        buf = steps[e]
        return pltpu.make_async_remote_copy(
            src_ref=buf.at[pl.ds(H, H)], dst_ref=buf.at[pl.ds(rows + H, H)],
            send_sem=send_sem.at[e, 0], recv_sem=recv_sem.at[e, 0],
            device_id={"gy": gy - 1}, device_id_type=pl.DeviceIdType.MESH)

    def to_right(e):
        buf = steps[e]
        return pltpu.make_async_remote_copy(
            src_ref=buf.at[pl.ds(rows, H)], dst_ref=buf.at[pl.ds(0, H)],
            send_sem=send_sem.at[e, 1], recv_sem=recv_sem.at[e, 1],
            device_id={"gy": gy + 1}, device_id_type=pl.DeviceIdType.MESH)

    def send(e):
        @pl.when(has_left)
        def _():
            to_left(e).start()

        @pl.when(has_right)
        def _():
            to_right(e).start()

    def receive(e):
        @pl.when(has_right)
        def _():
            to_left(e).wait_recv()

        @pl.when(has_left)
        def _():
            to_right(e).wait_recv()

    def turn(src, put):
        acc[0] = src[...].astype(F32)

        @pl.loop(0, rows)
        def _(y):
            put(y, acc[0, pl.ds(y, span, stride=rows), :])

    mask = maskp[...]

    def into(buf):
        def put(y, u):
            buf[y + H] = (u * mask).astype(buf.dtype)
        return put

    def put_speed(y, u):
        sq[y] = u * u * mask * (1.0 / 5040.0)

    turn(dens, into(den))
    send(0)
    turn(fnow, into(p0))
    send(1)
    turn(anow, into(q3))
    send(2)
    turn(fprev, into(p1))
    turn(anext, into(q2))
    turn(speed, put_speed)

    source_x, source_y, source_z = scal[0], scal[1], scal[2]
    at_x = lax.broadcasted_iota(jnp.int32, (span, depth), 0).astype(F32) == source_x
    at_z = lax.broadcasted_iota(jnp.int32, (span, depth), 1).astype(F32) == source_z
    hot[...] = jnp.where(at_x & at_z, mask, 0.0)
    nrec = recz.shape[0]
    mask2 = jnp.concatenate([mask[:half]] * (nrec // depth), axis=1)

    @pl.loop(0, rows)
    def _(y):
        lanes = lax.broadcasted_iota(jnp.int32, (nrec, half), 1) + y * half
        xt[y] = jnp.where(lanes == code_col[...], 1.0, 0.0).astype(BF)
        subs = lax.broadcasted_iota(jnp.int32, (half, nrec), 0) + y * half
        xo[y] = jnp.where(subs == code_row[...], mask2, 0.0).astype(BF)

    def planes(first, receive_from, body):
        @pl.loop(H, rows - H)
        def _(y):
            body(y)

        receive(receive_from)

        @pl.loop(0, 2 * H)
        def _(k):
            body(k + (rows - 2 * H) * (k // H))

    def slope(y):
        u = den[y + H]
        grad[0, y] = dot(dx[0:span, :], u) * (6.0 / 840.0)
        grad[2, y] = dot(u, mz[0:depth, 0:depth]) * (6.0 / 840.0)
        total = jnp.zeros((span, depth), F32)
        for k in range(1, 5):
            total = total + FIRST[k - 1] * (den[y + H + k].astype(F32) - den[y + H - k].astype(F32))
        grad[1, y] = total * (6.0 / 840.0)

    planes(0, 0, slope)

    def spatial(buf, y, exact, finish):
        u = buf[y + H]
        if exact:
            hi = u.astype(BF)
            along_z = dot(hi, mz[0:depth, :])
            along_x = dot(dx[...], hi)
        else:
            both = jnp.concatenate(split(u), axis=1)
            along_z = dot(both, mz[...])
            along_x = dot(dx[...], both)
        for r in range(0, span, CHUNK):
            rs = slice(r, r + CHUNK)
            first_x = along_x[rs, 0:depth]
            second_x = along_x[span + r : span + r + CHUNK, 0:depth]
            if not exact:
                first_x = first_x + along_x[rs, depth:]
                second_x = second_x + along_x[span + r : span + r + CHUNK, depth:]
            center = buf[y + H, rs, :]
            lap = (3.0 * SECOND[0]) * center + second_x + along_z[rs, depth:]
            slope_y = None
            for k in range(1, 5):
                up = buf[y + H + k, rs, :]
                down = buf[y + H - k, rs, :]
                lap = lap + SECOND[k] * (up + down)
                term = FIRST[k - 1] * (up - down)
                slope_y = term if slope_y is None else slope_y + term
            adv = (
                grad[0, y, rs, :] * first_x
                + grad[1, y, rs, :] * slope_y
                + grad[2, y, rs, :] * along_z[rs, 0:depth]
            )
            finish(r, rs, center, sq[y, rs, :] * (lap - adv))

    def acc_rows(t, y, r):
        return acc.at[t, pl.ds(pl.multiple_of(y * span + r, CHUNK), CHUNK), :]

    pressures = (p0, p1, p2)
    for t in range(NT):
        cur = pressures[t]
        vsum[...] = jnp.zeros_like(vsum)

        def forward(y, t=t, cur=cur):
            amount = jnp.where(y.astype(F32) == source_y, scal[3 + t], 0.0)
            pieces = []

            def finish(r, rs, center, lu):
                value = lu + amount * hot[rs, :]
                acc_rows(t, y, r)[...] = value
                old = p1[y + H, rs, :] if t == 0 else pressures[t - 1][y + H, rs, :]
                new = 2.0 * center - old + value
                if t < NT - 1:
                    pressures[t + 1][y + H, rs, :] = new
                if r < half:
                    pieces.append(new)

            spatial(cur, y, t == 0, finish)
            read = dot(xt[y], jnp.concatenate(split(jnp.concatenate(pieces, axis=0)), axis=1))
            vsum[...] += read[:, 0:depth] + read[:, depth:]

        planes(0, (1, 3, 4)[t], forward)
        if t < NT - 1:
            send(3 + t)
        here = lax.broadcasted_iota(jnp.int32, (nrec, depth), 1) == recz[...]
        residual = jnp.where(here, vsum[...] - obs[t], 0.0)
        hi, lo = split(residual)
        inj[t, :, 0:depth] = hi
        inj[t, :, depth:] = lo

    adjoint = {3: q3, 2: q2, 1: q1}
    for t in reversed(range(NT)):
        cur = adjoint[t + 1]

        def backward(y, t=t, cur=cur):
            added = dot(xo[y], inj[t])
            added = added[:, 0:depth] + added[:, depth:]
            images = []

            def finish(r, rs, center, lu):
                old = q2[y + H, rs, :] if t == NT - 1 else adjoint[t + 2][y + H, rs, :]
                new = 2.0 * center - old + lu
                if r < half:
                    new = new + added[rs]
                if t > 0:
                    adjoint[t][y + H, rs, :] = new
                term = new * acc_rows(t, y, r)[...]
                if t < NT - 1:
                    term = term + acc_rows(t + 1, y, r)[...]
                if t > 0:
                    acc_rows(t, y, r)[...] = term
                else:
                    images.append(term)

            spatial(cur, y, t == NT - 1, finish)
            if t == 0:
                out[y] = jnp.concatenate(images, axis=0).T

        planes(0, (6, 5, 2)[t], backward)
        if t > 0:
            send(5 + NT - 1 - t)

    for e in range(7):
        @pl.when(has_left)
        def _():
            to_left(e).wait_send()

        @pl.when(has_right)
        def _():
            to_right(e).wait_send()


def smooth_kernel(dims, starts, place, images, out, field, dist):
    shots, rows, layers, span, cells = dims
    for s in range(shots):
        window = images[s].reshape(rows * layers, span)
        if cells > span:
            window = jnp.concatenate([window, jnp.zeros((rows * layers, cells - span), F32)], axis=1)
        window = pltpu.roll(window, starts[s] * CX, 1)
        for c in range(cells // 128):
            piece = window[:, c * 128 : (c + 1) * 128]
            if s == 0:
                field[c] = piece
            else:
                field[c] += piece
    dist[...] = jnp.abs(
        lax.broadcasted_iota(jnp.int32, (cells, cells), 0) - lax.broadcasted_iota(jnp.int32, (cells, cells), 1)
    ).astype(F32)

    @pl.loop(0, layers)
    def _(z):
        depth_value = (place[0] * layers + z).astype(F32)
        length = CX * (1.5 + 4.5 * depth_value / (NZ - 1.0))
        rate = -1.0 / jnp.full((8, 128), length, F32)
        rate = rate[0:1, 0:1]
        weights = jnp.exp(dist[...] * rate)
        norm = jnp.sum(weights, axis=0, keepdims=True)
        w_hi, w_lo = split(weights)
        layer = jnp.concatenate(
            [field[c, pl.ds(z, rows, stride=layers), :] for c in range(cells // 128)], axis=1
        )
        f_hi, f_lo = split(layer)
        main = dot(jnp.concatenate([f_hi, f_lo], axis=0), w_hi)
        total = main[0:rows] + main[rows:] + dot(f_hi, w_lo)
        out[z] = total / norm


def on_device(
    velocity, log_density, fwd_prev, fwd_now, adj_now, adj_next,
    wavelet, source_pos, receiver_pos, observed, footprint, owner,
):
    shot = lax.axis_index("gx")
    column_index = lax.axis_index("gy")
    block_count = lax.axis_size("gx")
    block_cells, rows, depth = velocity.shape[1:]
    slots = footprint.shape[1]
    span = slots * block_cells
    half = span // 2
    speeds = lax.all_gather(velocity, "gx", axis=0, tiled=True)
    densities = lax.all_gather(log_density, "gx", axis=0, tiled=True)
    blocks = footprint[shot]
    holders = owner[jnp.maximum(blocks, 0)]
    speed = speeds[holders].reshape(span * rows, depth)
    dens = densities[holders].reshape(span * rows, depth)
    mask = jnp.broadcast_to(
        jnp.repeat((blocks >= 0).astype(F32), block_cells)[:, None], (span, depth)
    )
    spot = source_pos[0] - jnp.stack([jnp.int32(0), column_index * rows, jnp.int32(0)])
    scal = jnp.concatenate([spot.astype(F32), wavelet[0]])
    rec_y = receiver_pos[0, 1] - column_index * rows
    valid = (rec_y >= 0) & (rec_y < rows)
    code = jnp.where(valid, rec_y * half + receiver_pos[0, 0], -1)
    nrec = code.shape[0]
    first_x, second_x = band(span)
    first_z, second_z = band(depth)
    dx = jnp.asarray(np.concatenate([first_x, second_x], 0), BF)
    one = np.concatenate([first_z.T, second_z.T], 1)
    mz = jnp.asarray(np.concatenate([one, one], 0), BF)
    flat = lambda a: a.reshape(span * rows, depth)
    vm = pl.BlockSpec(memory_space=pltpu.VMEM)
    padded = pltpu.VMEM((rows + 2 * H, span, depth), F32)
    out = pl.pallas_call(
        functools.partial(wave_kernel, (rows, span, depth)),
        out_shape=jax.ShapeDtypeStruct((rows, depth, span), F32),
        in_specs=[pl.BlockSpec(memory_space=pltpu.SMEM)] + [vm] * 13,
        out_specs=vm,
        scratch_shapes=[
            padded, padded, padded, padded, padded, padded,
            pltpu.VMEM((NT, rows * span, depth), F32),
            pltpu.VMEM((rows, span, depth), F32),
            pltpu.VMEM((3, rows, span, depth), F32),
            pltpu.VMEM((rows + 2 * H, span, depth), BF),
            pltpu.VMEM((rows, nrec, half), BF),
            pltpu.VMEM((rows, half, nrec), BF),
            pltpu.VMEM((span, depth), F32),
            pltpu.VMEM((nrec, depth), F32),
            pltpu.VMEM((NT, nrec, 2 * depth), BF),
            pltpu.SemaphoreType.DMA((7, 2)),
            pltpu.SemaphoreType.DMA((7, 2)),
        ],
        compiler_params=pltpu.CompilerParams(
            collective_id=0, has_side_effects=True, vmem_limit_bytes=60 * 1024 * 1024
        ),
        name="wave",
    )(
        scal, flat(fwd_prev), flat(fwd_now), flat(adj_now), flat(adj_next), speed, dens, mask,
        code[:, None], code[None, :], receiver_pos[0, 2][:, None], observed[0][:, :, None], dx, mz,
    )
    layers = depth // block_count
    received = lax.all_to_all(out, "gx", split_axis=1, concat_axis=0, tiled=True)
    received = received.reshape(block_count, rows, layers, span)
    cells = block_count * block_cells
    shots = footprint.shape[0]
    sm = pl.BlockSpec(memory_space=pltpu.SMEM)
    return pl.pallas_call(
        functools.partial(smooth_kernel, (shots, rows, layers, span, cells)),
        out_shape=jax.ShapeDtypeStruct((layers, rows, cells), F32),
        in_specs=[sm, sm, vm],
        out_specs=vm,
        scratch_shapes=[
            pltpu.VMEM((cells // 128, rows * layers, 128), F32),
            pltpu.VMEM((cells, cells), F32),
        ],
        compiler_params=pltpu.CompilerParams(vmem_limit_bytes=56 * 1024 * 1024),
        name="smooth",
    )(footprint[:, 0], shot[None], received)


def solution(mesh):
    shared = P(("grp", "gx"), None, "gy", None)
    placed = (shared,) * 6 + (
        P(("grp", "gx"), None),
        P(("grp", "gx"), None),
        P(("grp", "gx"), None, None),
        P(("grp", "gx"), None, None),
        P("grp", None),
        P(),
    )
    return jax.shard_map(
        on_device,
        mesh=mesh,
        in_specs=placed,
        out_specs=P(("grp", "gx"), "gy", None),
        check_vma=False,
    )
```

```python
import functools

import jax
import jax.numpy as jnp
import numpy as np
from jax import lax
from jax.experimental import pallas as pl
from jax.experimental.pallas import tpu as pltpu
from jax.sharding import PartitionSpec as P

CX = 64
NZ = 128
NT = 3
H = 4
SECOND = (-14350.0, 8064.0, -1008.0, 128.0, -9.0)
FIRST = (672.0, -168.0, 32.0, -3.0)
BF = jnp.bfloat16
F32 = jnp.float32
CHUNK = 32


def band(size):
    first = np.zeros((size, size), np.float32)
    second = np.zeros((size, size), np.float32)
    for k in range(1, 5):
        ahead = np.eye(size, k=k, dtype=np.float32)
        first += FIRST[k - 1] * (ahead - ahead.T)
        second += SECOND[k] * (ahead + ahead.T)
    return first, second


def dot(a, b):
    return jnp.dot(a, b, preferred_element_type=F32)


def split(u):
    hi = u.astype(BF)
    return hi, (u - hi.astype(F32)).astype(BF)


def wave_kernel(
    dims,
    source_pos, wavelet, footprint, owner,
    fprev, fnow, anow, anext, speed, dens, receivers, observed, dx, mz,
    out,
    p0, p1, p2, q3, q2, q1, acc, sq, grad, den, xt, xo, hot, vsum, inj,
    model_d, model_s, maskp, obs, recz, outb,
    send_sem, recv_sem, model_send, model_recv, image_send, image_recv, own_sem,
):
    rows, span, depth, cells = dims
    half = span // 2
    gx = lax.axis_index("gx")
    lanes_gx = lax.axis_size("gx")
    gy = lax.axis_index("gy")
    count = lax.axis_size("gy")
    layers = depth // lanes_gx
    has_left = gy > 0
    has_right = gy < count - 1
    barrier = pltpu.get_barrier_semaphore()
    steps = (den, p0, q3, p1, p2, q2, q1)

    for d in range(1, lanes_gx):
        pl.semaphore_signal(
            barrier, inc=1, device_id={"gx": lax.rem(gx + d, lanes_gx)}, device_id_type=pl.DeviceIdType.MESH
        )

    @pl.when(has_left)
    def _():
        pl.semaphore_signal(barrier, inc=1, device_id={"gy": gy - 1}, device_id_type=pl.DeviceIdType.MESH)

    @pl.when(has_right)
    def _():
        pl.semaphore_signal(barrier, inc=1, device_id={"gy": gy + 1}, device_id_type=pl.DeviceIdType.MESH)

    model = (model_d, model_s)
    model_d[gx] = dens[...]
    model_s[gx] = speed[...]

    @pl.when(jnp.logical_not(has_left))
    def _():
        for buf in steps:
            buf[0:H] = jnp.zeros((H, span, depth), buf.dtype)

    @pl.when(jnp.logical_not(has_right))
    def _():
        for buf in steps:
            buf[rows + H : rows + 2 * H] = jnp.zeros((H, span, depth), buf.dtype)

    pl.semaphore_wait(
        barrier, lanes_gx - 1 + has_left.astype(jnp.int32) + has_right.astype(jnp.int32)
    )

    def up_copy(a, r, block):
        return pltpu.make_async_remote_copy(
            src_ref=model[a].at[block], dst_ref=model[a].at[block],
            send_sem=model_send.at[a, 0, r], recv_sem=model_recv.at[a, 0, r],
            device_id={"gx": gx + 1}, device_id_type=pl.DeviceIdType.MESH)

    def down_copy(a, r, block):
        return pltpu.make_async_remote_copy(
            src_ref=model[a].at[block], dst_ref=model[a].at[block],
            send_sem=model_send.at[a, 1, r], recv_sem=model_recv.at[a, 1, r],
            device_id={"gx": gx - 1}, device_id_type=pl.DeviceIdType.MESH)

    def pass_on(a, r):
        @pl.when((gx - r >= 0) & (gx + 1 < lanes_gx))
        def _():
            up_copy(a, r, gx - r).start()

        @pl.when((gx + r < lanes_gx) & (gx >= 1))
        def _():
            down_copy(a, r, gx + r).start()

    def passed(a, r):
        @pl.when((gx - r >= 0) & (gx + 1 < lanes_gx))
        def _():
            up_copy(a, r, gx - r).wait_send()

        @pl.when((gx + r < lanes_gx) & (gx >= 1))
        def _():
            down_copy(a, r, gx + r).wait_send()

    def arrive(a, r):
        @pl.when(gx - 1 - r >= 0)
        def _():
            up_copy(a, r, gx - 1 - r).wait_recv()

        @pl.when(gx + 1 + r < lanes_gx)
        def _():
            down_copy(a, r, gx + 1 + r).wait_recv()

    pass_on(0, 0)
    pass_on(1, 0)

    def to_left(e):
        buf = steps[e]
        return pltpu.make_async_remote_copy(
            src_ref=buf.at[pl.ds(H, H)], dst_ref=buf.at[pl.ds(rows + H, H)],
            send_sem=send_sem.at[e, 0], recv_sem=recv_sem.at[e, 0],
            device_id={"gy": gy - 1}, device_id_type=pl.DeviceIdType.MESH)

    def to_right(e):
        buf = steps[e]
        return pltpu.make_async_remote_copy(
            src_ref=buf.at[pl.ds(rows, H)], dst_ref=buf.at[pl.ds(0, H)],
            send_sem=send_sem.at[e, 1], recv_sem=recv_sem.at[e, 1],
            device_id={"gy": gy + 1}, device_id_type=pl.DeviceIdType.MESH)

    def send(e):
        @pl.when(has_left)
        def _():
            to_left(e).start()

        @pl.when(has_right)
        def _():
            to_right(e).start()

    def receive(e):
        @pl.when(has_right)
        def _():
            to_left(e).wait_recv()

        @pl.when(has_left)
        def _():
            to_right(e).wait_recv()

    def turn(src, put):
        acc[0] = src[...].astype(F32)

        @pl.loop(0, rows)
        def _(y):
            put(y, acc[0, pl.ds(y, span, stride=rows), :])

    slots = footprint.shape[1]
    block_rows = dens.shape[0]
    lives = [footprint[gx, j] for j in range(slots)]
    for j in range(slots):
        live = jnp.where(lives[j] >= 0, 1.0, 0.0)
        maskp[j * cells : (j + 1) * cells] = jnp.full((cells, depth), live, F32)
    mask = maskp[...]

    def into(buf):
        def put(y, u):
            buf[y + H] = (u * mask).astype(buf.dtype)
        return put

    def put_speed(y, u):
        sq[y] = u * u * mask * (1.0 / 5040.0)

    def gather(a, put):
        for j in range(slots):
            holder = owner[jnp.maximum(lives[j], 0)]
            acc[0, j * block_rows : (j + 1) * block_rows] = model[a][holder].astype(F32)

        @pl.loop(0, rows)
        def _(y):
            put(y, acc[0, pl.ds(y, span, stride=rows), :])

    turn(fnow, into(p0))
    send(1)
    turn(anow, into(q3))
    send(2)

    def onward(r):
        for a in range(2):
            arrive(a, r - 1)
            pass_on(a, r)

    nrec = receivers.shape[1]

    def column(row):
        return jnp.broadcast_to(row.astype(F32), (depth, nrec)).T

    for t in range(NT):
        obs[t] = column(observed[t : t + 1, :])
    recz[...] = column(receivers[2:3, :])
    rec_y = receivers[1:2, :] - gy * rows
    valid = (rec_y >= 0) & (rec_y < rows)
    code_row = jnp.where(valid, rec_y * half + receivers[0:1, :], -1)
    code_col = column(code_row)
    source_x = source_pos[0, 0].astype(F32)
    source_y = (source_pos[0, 1] - gy * rows).astype(F32)
    source_z = source_pos[0, 2].astype(F32)
    at_x = lax.broadcasted_iota(jnp.int32, (span, depth), 0).astype(F32) == source_x
    at_z = lax.broadcasted_iota(jnp.int32, (span, depth), 1).astype(F32) == source_z
    hot[...] = jnp.where(at_x & at_z, mask, 0.0)
    mask2 = jnp.concatenate([mask[:half]] * (nrec // depth), axis=1)
    code_lanes = jnp.concatenate([code_col] * (half // depth), axis=1)

    @pl.loop(0, rows)
    def _(y):
        lanes = (lax.broadcasted_iota(jnp.int32, (nrec, half), 1) + y * half).astype(F32)
        xt[y] = jnp.where(lanes == code_lanes, 1.0, 0.0).astype(BF)
        subs = lax.broadcasted_iota(jnp.int32, (half, nrec), 0) + y * half
        xo[y] = jnp.where(subs == code_row, mask2, 0.0).astype(BF)

    onward(1)
    turn(fprev, into(p1))
    turn(anext, into(q2))
    for r in range(2, lanes_gx - 1):
        onward(r)
    arrive(0, lanes_gx - 2)
    gather(0, into(den))
    send(0)

    def planes(first, receive_from, body, after=None):
        @pl.loop(H, rows - H)
        def _(y):
            body(y)

        if after is not None:
            after()
        receive(receive_from)

        @pl.loop(0, 2 * H)
        def _(k):
            body(k + (rows - 2 * H) * (k // H))

    def slope(y):
        u = den[y + H]
        grad[0, y] = dot(dx[0:span, :], u) * (6.0 / 840.0)
        grad[2, y] = dot(u, mz[0:depth, 0:depth]) * (6.0 / 840.0)
        total = jnp.zeros((span, depth), F32)
        for k in range(1, 5):
            total = total + FIRST[k - 1] * (den[y + H + k].astype(F32) - den[y + H - k].astype(F32))
        grad[1, y] = total * (6.0 / 840.0)

    planes(0, 0, slope)
    arrive(1, lanes_gx - 2)
    gather(1, put_speed)

    def spatial(buf, y, exact, finish):
        u = buf[y + H]
        if exact:
            hi = u.astype(BF)
            along_z = dot(hi, mz[0:depth, :])
            along_x = dot(dx[...], hi)
        else:
            both = jnp.concatenate(split(u), axis=1)
            along_z = dot(both, mz[...])
            along_x = dot(dx[...], both)
        for r in range(0, span, CHUNK):
            rs = slice(r, r + CHUNK)
            first_x = along_x[rs, 0:depth]
            second_x = along_x[span + r : span + r + CHUNK, 0:depth]
            if not exact:
                first_x = first_x + along_x[rs, depth:]
                second_x = second_x + along_x[span + r : span + r + CHUNK, depth:]
            center = buf[y + H, rs, :]
            lap = (3.0 * SECOND[0]) * center + second_x + along_z[rs, depth:]
            slope_y = None
            for k in range(1, 5):
                up = buf[y + H + k, rs, :]
                down = buf[y + H - k, rs, :]
                lap = lap + SECOND[k] * (up + down)
                term = FIRST[k - 1] * (up - down)
                slope_y = term if slope_y is None else slope_y + term
            adv = (
                grad[0, y, rs, :] * first_x
                + grad[1, y, rs, :] * slope_y
                + grad[2, y, rs, :] * along_z[rs, 0:depth]
            )
            finish(r, rs, center, sq[y, rs, :] * (lap - adv))

    def acc_rows(t, y, r):
        return acc.at[t, pl.ds(pl.multiple_of(y * span + r, CHUNK), CHUNK), :]

    pressures = (p0, p1, p2)
    for t in range(NT):
        cur = pressures[t]
        vsum[...] = jnp.zeros_like(vsum)

        def forward(y, t=t, cur=cur):
            amount = jnp.where(y.astype(F32) == source_y, wavelet[0, t], 0.0)
            pieces = []

            def finish(r, rs, center, lu):
                value = lu + amount * hot[rs, :]
                acc_rows(t, y, r)[...] = value
                old = p1[y + H, rs, :] if t == 0 else pressures[t - 1][y + H, rs, :]
                new = 2.0 * center - old + value
                if t < NT - 1:
                    pressures[t + 1][y + H, rs, :] = new
                if r < half:
                    pieces.append(new)

            spatial(cur, y, t == 0, finish)
            read = dot(xt[y], jnp.concatenate(split(jnp.concatenate(pieces, axis=0)), axis=1))
            vsum[...] += read[:, 0:depth] + read[:, depth:]

        planes(0, (1, 3, 4)[t], forward)
        if t < NT - 1:
            send(3 + t)
        here = lax.broadcasted_iota(jnp.int32, (nrec, depth), 1).astype(F32) == recz[...]
        residual = jnp.where(here, vsum[...] - obs[t], 0.0)
        hi, lo = split(residual)
        inj[t, :, 0:depth] = hi
        inj[t, :, depth:] = lo

    parts = ((H, rows - 2 * H), (0, H), (rows - H, H))

    def image_copy(d, part, target):
        start, size = parts[part]
        return pltpu.make_async_remote_copy(
            src_ref=outb.at[pl.ds(start, size), pl.ds(pl.multiple_of(target * layers, layers), layers), :],
            dst_ref=out.at[gx, pl.ds(start, size)],
            send_sem=image_send.at[d, part], recv_sem=image_recv.at[d, part],
            device_id={"gx": target}, device_id_type=pl.DeviceIdType.MESH)

    def deliver(part):
        for d in range(1, lanes_gx):
            image_copy(d, part, lax.rem(gx + d, lanes_gx)).start()

    def delivered(part):
        for d in range(1, lanes_gx):
            copy = image_copy(d, part, lax.rem(gx + d, lanes_gx))
            copy.wait_send()
            start, size = parts[part]
            came = lax.rem(gx + lanes_gx - d, lanes_gx)
            pltpu.make_async_remote_copy(
                src_ref=outb.at[pl.ds(start, size), pl.ds(pl.multiple_of(gx * layers, layers), layers), :],
                dst_ref=out.at[came, pl.ds(start, size)],
                send_sem=image_send.at[d, part], recv_sem=image_recv.at[d, part],
                device_id={"gx": came}, device_id_type=pl.DeviceIdType.MESH).wait_recv()

    adjoint = {3: q3, 2: q2, 1: q1}
    for t in reversed(range(NT)):
        cur = adjoint[t + 1]

        def backward(y, t=t, cur=cur):
            added = dot(xo[y], inj[t])
            added = added[:, 0:depth] + added[:, depth:]
            images = []

            def finish(r, rs, center, lu):
                old = q2[y + H, rs, :] if t == NT - 1 else adjoint[t + 2][y + H, rs, :]
                new = 2.0 * center - old + lu
                if r < half:
                    new = new + added[rs]
                if t > 0:
                    adjoint[t][y + H, rs, :] = new
                term = new * acc_rows(t, y, r)[...]
                if t < NT - 1:
                    term = term + acc_rows(t + 1, y, r)[...]
                if t > 0:
                    acc_rows(t, y, r)[...] = term
                else:
                    images.append(term)

            spatial(cur, y, t == NT - 1, finish)
            if t == 0:
                outb[y] = jnp.concatenate(images, axis=0).T

        planes(0, (6, 5, 2)[t], backward, None if t > 0 else functools.partial(deliver, 0))
        if t > 0:
            send(5 + NT - 1 - t)

    deliver(1)
    deliver(2)
    own = pltpu.make_async_copy(
        outb.at[:, pl.ds(pl.multiple_of(gx * layers, layers), layers), :], out.at[gx], own_sem
    )
    own.start()
    for r in range(lanes_gx - 1):
        passed(0, r)
        passed(1, r)
    for e in range(7):
        @pl.when(has_left)
        def _():
            to_left(e).wait_send()

        @pl.when(has_right)
        def _():
            to_right(e).wait_send()

    own.wait()
    for part in range(len(parts)):
        delivered(part)


def smooth_kernel(dims, footprint, images, out, field, dist):
    shots, rows, layers, span, cells = dims
    place = lax.axis_index("gx")
    for s in range(shots):
        window = images[s].reshape(rows * layers, span)
        if cells > span:
            window = jnp.concatenate([window, jnp.zeros((rows * layers, cells - span), F32)], axis=1)
        window = pltpu.roll(window, footprint[s, 0] * CX, 1)
        for c in range(cells // 128):
            piece = window[:, c * 128 : (c + 1) * 128]
            if s == 0:
                field[c] = piece
            else:
                field[c] += piece
    dist[...] = jnp.abs(
        lax.broadcasted_iota(jnp.int32, (cells, cells), 0) - lax.broadcasted_iota(jnp.int32, (cells, cells), 1)
    ).astype(F32)

    @pl.loop(0, layers)
    def _(z):
        depth_value = (place * layers + z).astype(F32)
        length = CX * (1.5 + 4.5 * depth_value / (NZ - 1.0))
        rate = -1.0 / jnp.full((8, 128), length, F32)
        rate = rate[0:1, 0:1]
        weights = jnp.exp(dist[...] * rate)
        norm = jnp.sum(weights, axis=0, keepdims=True)
        w_hi, w_lo = split(weights)
        layer = jnp.concatenate(
            [field[c, pl.ds(z, rows, stride=layers), :] for c in range(cells // 128)], axis=1
        )
        f_hi, f_lo = split(layer)
        main = dot(jnp.concatenate([f_hi, f_lo], axis=0), w_hi)
        total = main[0:rows] + main[rows:] + dot(f_hi, w_lo)
        out[z] = total / norm


def on_device(
    velocity, log_density, fwd_prev, fwd_now, adj_now, adj_next,
    wavelet, source_pos, receiver_pos, observed, footprint, owner,
):
    block_count = lax.axis_size("gx")
    block_cells, rows, depth = velocity.shape[1:]
    shots, slots = footprint.shape
    span = slots * block_cells
    half = span // 2
    layers = depth // block_count
    nrec = receiver_pos.shape[2]
    first_x, second_x = band(span)
    first_z, second_z = band(depth)
    dx = jnp.asarray(np.concatenate([first_x, second_x], 0), BF)
    one = np.concatenate([first_z.T, second_z.T], 1)
    mz = jnp.asarray(np.concatenate([one, one], 0), BF)
    flat = lambda a: a.reshape(a.shape[1] * rows, depth)
    vm = pl.BlockSpec(memory_space=pltpu.VMEM)
    sm = pl.BlockSpec(memory_space=pltpu.SMEM)
    padded = pltpu.VMEM((rows + 2 * H, span, depth), F32)
    received = pl.pallas_call(
        functools.partial(wave_kernel, (rows, span, depth, block_cells)),
        out_shape=jax.ShapeDtypeStruct((block_count, rows, layers, span), F32),
        in_specs=[sm] * 4 + [vm] * 10,
        out_specs=pl.BlockSpec(memory_space=pl.ANY),
        scratch_shapes=[
            padded, padded, padded, padded, padded, padded,
            pltpu.VMEM((NT, rows * span, depth), F32),
            pltpu.VMEM((rows, span, depth), F32),
            pltpu.VMEM((3, rows, span, depth), F32),
            pltpu.VMEM((rows + 2 * H, span, depth), BF),
            pltpu.VMEM((rows, nrec, half), BF),
            pltpu.VMEM((rows, half, nrec), BF),
            pltpu.VMEM((span, depth), F32),
            pltpu.VMEM((nrec, depth), F32),
            pltpu.VMEM((NT, nrec, 2 * depth), BF),
            pltpu.VMEM((block_count, block_cells * rows, depth), BF),
            pltpu.VMEM((block_count, block_cells * rows, depth), BF),
            pltpu.VMEM((span, depth), F32),
            pltpu.VMEM((NT, nrec, depth), F32),
            pltpu.VMEM((nrec, depth), F32),
            pltpu.VMEM((rows, depth, span), F32),
            pltpu.SemaphoreType.DMA((7, 2)),
            pltpu.SemaphoreType.DMA((7, 2)),
            pltpu.SemaphoreType.DMA((2, 2, block_count)),
            pltpu.SemaphoreType.DMA((2, 2, block_count)),
            pltpu.SemaphoreType.DMA((block_count, 3)),
            pltpu.SemaphoreType.DMA((block_count, 3)),
            pltpu.SemaphoreType.DMA,
        ],
        compiler_params=pltpu.CompilerParams(
            collective_id=0, has_side_effects=True, vmem_limit_bytes=60 * 1024 * 1024
        ),
        name="wave",
    )(
        source_pos, wavelet, footprint, owner,
        flat(fwd_prev), flat(fwd_now), flat(adj_now), flat(adj_next), flat(velocity), flat(log_density),
        receiver_pos[0], observed[0], dx, mz,
    )
    cells = block_count * block_cells
    return pl.pallas_call(
        functools.partial(smooth_kernel, (shots, rows, layers, span, cells)),
        out_shape=jax.ShapeDtypeStruct((layers, rows, cells), F32),
        in_specs=[sm, vm],
        out_specs=vm,
        scratch_shapes=[
            pltpu.VMEM((cells // 128, rows * layers, 128), F32),
            pltpu.VMEM((cells, cells), F32),
        ],
        compiler_params=pltpu.CompilerParams(vmem_limit_bytes=56 * 1024 * 1024),
        name="smooth",
    )(footprint, received)


def solution(mesh):
    shared = P(("grp", "gx"), None, "gy", None)
    placed = (shared,) * 6 + (
        P(("grp", "gx"), None),
        P(("grp", "gx"), None),
        P(("grp", "gx"), None, None),
        P(("grp", "gx"), None, None),
        P("grp", None),
        P(),
    )
    return jax.shard_map(
        on_device,
        mesh=mesh,
        in_specs=placed,
        out_specs=P(("grp", "gx"), "gy", None),
        check_vma=False,
    )
```

```python
import functools

import jax
import jax.numpy as jnp
import numpy as np
from jax import lax
from jax.experimental import pallas as pl
from jax.experimental.pallas import tpu as pltpu
from jax.sharding import PartitionSpec as P

CX = 64
NZ = 128
NT = 3
H = 4
SECOND = (-14350.0, 8064.0, -1008.0, 128.0, -9.0)
FIRST = (672.0, -168.0, 32.0, -3.0)
BF = jnp.bfloat16
F32 = jnp.float32
CHUNK = 32


def band(size):
    first = np.zeros((size, size), np.float32)
    second = np.zeros((size, size), np.float32)
    for k in range(1, 5):
        ahead = np.eye(size, k=k, dtype=np.float32)
        first += FIRST[k - 1] * (ahead - ahead.T)
        second += SECOND[k] * (ahead + ahead.T)
    return first, second


def dot(a, b):
    return jnp.dot(a, b, preferred_element_type=F32)


def split(u):
    hi = u.astype(BF)
    return hi, (u - hi.astype(F32)).astype(BF)


def wave_kernel(
    dims,
    source_pos, wavelet, footprint, owner,
    fprev, fnow, anow, anext, speed, dens, receivers, observed, dx, mz,
    out, tails,
    p0, p1, p2, q3, q2, q1, acc, sq, grad, den, xt, xo, hot, vsum, inj,
    model_d, model_s, maskp, obs, recz, outb, carry, tailb,
    send_sem, recv_sem, model_send, model_recv, image_send, image_recv, own_sem, own_tail,
):
    rows, span, depth, cells = dims
    half = span // 2
    gx = lax.axis_index("gx")
    lanes_gx = lax.axis_size("gx")
    gy = lax.axis_index("gy")
    count = lax.axis_size("gy")
    layers = depth // lanes_gx
    has_left = gy > 0
    has_right = gy < count - 1
    barrier = pltpu.get_barrier_semaphore()
    steps = (den, p0, q3, p1, p2, q2, q1)

    for d in range(1, lanes_gx):
        pl.semaphore_signal(
            barrier, inc=1, device_id={"gx": lax.rem(gx + d, lanes_gx)}, device_id_type=pl.DeviceIdType.MESH
        )

    @pl.when(has_left)
    def _():
        pl.semaphore_signal(barrier, inc=1, device_id={"gy": gy - 1}, device_id_type=pl.DeviceIdType.MESH)

    @pl.when(has_right)
    def _():
        pl.semaphore_signal(barrier, inc=1, device_id={"gy": gy + 1}, device_id_type=pl.DeviceIdType.MESH)

    model = (model_d, model_s)
    model_d[gx] = dens[...]
    model_s[gx] = speed[...]

    @pl.when(jnp.logical_not(has_left))
    def _():
        for buf in steps:
            buf[0:H] = jnp.zeros((H, span, depth), buf.dtype)

    @pl.when(jnp.logical_not(has_right))
    def _():
        for buf in steps:
            buf[rows + H : rows + 2 * H] = jnp.zeros((H, span, depth), buf.dtype)

    pl.semaphore_wait(
        barrier, lanes_gx - 1 + has_left.astype(jnp.int32) + has_right.astype(jnp.int32)
    )

    def up_copy(a, r, block):
        return pltpu.make_async_remote_copy(
            src_ref=model[a].at[block], dst_ref=model[a].at[block],
            send_sem=model_send.at[a, 0, r], recv_sem=model_recv.at[a, 0, r],
            device_id={"gx": gx + 1}, device_id_type=pl.DeviceIdType.MESH)

    def down_copy(a, r, block):
        return pltpu.make_async_remote_copy(
            src_ref=model[a].at[block], dst_ref=model[a].at[block],
            send_sem=model_send.at[a, 1, r], recv_sem=model_recv.at[a, 1, r],
            device_id={"gx": gx - 1}, device_id_type=pl.DeviceIdType.MESH)

    def pass_on(a, r):
        @pl.when((gx - r >= 0) & (gx + 1 < lanes_gx))
        def _():
            up_copy(a, r, gx - r).start()

        @pl.when((gx + r < lanes_gx) & (gx >= 1))
        def _():
            down_copy(a, r, gx + r).start()

    def passed(a, r):
        @pl.when((gx - r >= 0) & (gx + 1 < lanes_gx))
        def _():
            up_copy(a, r, gx - r).wait_send()

        @pl.when((gx + r < lanes_gx) & (gx >= 1))
        def _():
            down_copy(a, r, gx + r).wait_send()

    def arrive(a, r):
        @pl.when(gx - 1 - r >= 0)
        def _():
            up_copy(a, r, gx - 1 - r).wait_recv()

        @pl.when(gx + 1 + r < lanes_gx)
        def _():
            down_copy(a, r, gx + 1 + r).wait_recv()

    pass_on(0, 0)
    pass_on(1, 0)

    def to_left(e):
        buf = steps[e]
        return pltpu.make_async_remote_copy(
            src_ref=buf.at[pl.ds(H, H)], dst_ref=buf.at[pl.ds(rows + H, H)],
            send_sem=send_sem.at[e, 0], recv_sem=recv_sem.at[e, 0],
            device_id={"gy": gy - 1}, device_id_type=pl.DeviceIdType.MESH)

    def to_right(e):
        buf = steps[e]
        return pltpu.make_async_remote_copy(
            src_ref=buf.at[pl.ds(rows, H)], dst_ref=buf.at[pl.ds(0, H)],
            send_sem=send_sem.at[e, 1], recv_sem=recv_sem.at[e, 1],
            device_id={"gy": gy + 1}, device_id_type=pl.DeviceIdType.MESH)

    def send(e):
        @pl.when(has_left)
        def _():
            to_left(e).start()

        @pl.when(has_right)
        def _():
            to_right(e).start()

    def receive(e):
        @pl.when(has_right)
        def _():
            to_left(e).wait_recv()

        @pl.when(has_left)
        def _():
            to_right(e).wait_recv()

    def turn(src, put):
        acc[0] = src[...].astype(F32)

        @pl.loop(0, rows)
        def _(y):
            put(y, acc[0, pl.ds(y, span, stride=rows), :])

    slots = footprint.shape[1]
    block_rows = dens.shape[0]
    lives = [footprint[gx, j] for j in range(slots)]
    for j in range(slots):
        live = jnp.where(lives[j] >= 0, 1.0, 0.0)
        maskp[j * cells : (j + 1) * cells] = jnp.full((cells, depth), live, F32)
    mask = maskp[...]

    def into(buf):
        def put(y, u):
            buf[y + H] = (u * mask).astype(buf.dtype)
        return put

    def put_speed(y, u):
        sq[y] = u * u * mask * (1.0 / 5040.0)

    def gather(a, put):
        for j in range(slots):
            holder = owner[jnp.maximum(lives[j], 0)]
            acc[0, j * block_rows : (j + 1) * block_rows] = model[a][holder].astype(F32)

        @pl.loop(0, rows)
        def _(y):
            put(y, acc[0, pl.ds(y, span, stride=rows), :])

    turn(fnow, into(p0))
    send(1)
    turn(anow, into(q3))
    send(2)

    def onward(r):
        for a in range(2):
            arrive(a, r - 1)
            pass_on(a, r)

    nrec = receivers.shape[1]

    def column(row):
        return jnp.broadcast_to(row.astype(F32), (depth, nrec)).T

    for t in range(NT):
        obs[t] = column(observed[t : t + 1, :])
    recz[...] = column(receivers[2:3, :])
    rec_y = receivers[1:2, :] - gy * rows
    valid = (rec_y >= 0) & (rec_y < rows)
    code_row = jnp.where(valid, rec_y * half + receivers[0:1, :], -1)
    code_col = column(code_row)
    source_x = source_pos[0, 0].astype(F32)
    source_y = (source_pos[0, 1] - gy * rows).astype(F32)
    source_z = source_pos[0, 2].astype(F32)
    at_x = lax.broadcasted_iota(jnp.int32, (span, depth), 0).astype(F32) == source_x
    at_z = lax.broadcasted_iota(jnp.int32, (span, depth), 1).astype(F32) == source_z
    hot[...] = jnp.where(at_x & at_z, mask, 0.0)
    mask2 = jnp.concatenate([mask[:half]] * (nrec // depth), axis=1)
    code_lanes = jnp.concatenate([code_col] * (half // depth), axis=1)

    @pl.loop(0, rows)
    def _(y):
        lanes = (lax.broadcasted_iota(jnp.int32, (nrec, half), 1) + y * half).astype(F32)
        xt[y] = jnp.where(lanes == code_lanes, 1.0, 0.0).astype(BF)
        subs = lax.broadcasted_iota(jnp.int32, (half, nrec), 0) + y * half
        xo[y] = jnp.where(subs == code_row, mask2, 0.0).astype(BF)

    onward(1)
    turn(fprev, into(p1))
    turn(anext, into(q2))
    for r in range(2, lanes_gx - 1):
        onward(r)
    arrive(0, lanes_gx - 2)
    gather(0, into(den))
    send(0)

    def planes(first, receive_from, body, after=None):
        @pl.loop(H, rows - H)
        def _(y):
            body(y)

        if after is not None:
            after()
        receive(receive_from)

        @pl.loop(0, 2 * H)
        def _(k):
            body(k + (rows - 2 * H) * (k // H))

    def slope(y):
        u = den[y + H]
        grad[0, y] = dot(dx[0:span, :], u) * (6.0 / 840.0)
        grad[2, y] = dot(u, mz[0:depth, 0:depth]) * (6.0 / 840.0)
        total = jnp.zeros((span, depth), F32)
        for k in range(1, 5):
            total = total + FIRST[k - 1] * (den[y + H + k].astype(F32) - den[y + H - k].astype(F32))
        grad[1, y] = total * (6.0 / 840.0)

    planes(0, 0, slope)
    arrive(1, lanes_gx - 2)
    gather(1, put_speed)

    def spatial(buf, y, exact, finish):
        u = buf[y + H]
        if exact:
            hi = u.astype(BF)
            along_z = dot(hi, mz[0:depth, :])
            along_x = dot(dx[...], hi)
        else:
            both = jnp.concatenate(split(u), axis=1)
            along_z = dot(both, mz[...])
            along_x = dot(dx[...], both)
        for r in range(0, span, CHUNK):
            rs = slice(r, r + CHUNK)
            first_x = along_x[rs, 0:depth]
            second_x = along_x[span + r : span + r + CHUNK, 0:depth]
            if not exact:
                first_x = first_x + along_x[rs, depth:]
                second_x = second_x + along_x[span + r : span + r + CHUNK, depth:]
            center = buf[y + H, rs, :]
            lap = (3.0 * SECOND[0]) * center + second_x + along_z[rs, depth:]
            slope_y = None
            for k in range(1, 5):
                up = buf[y + H + k, rs, :]
                down = buf[y + H - k, rs, :]
                lap = lap + SECOND[k] * (up + down)
                term = FIRST[k - 1] * (up - down)
                slope_y = term if slope_y is None else slope_y + term
            adv = (
                grad[0, y, rs, :] * first_x
                + grad[1, y, rs, :] * slope_y
                + grad[2, y, rs, :] * along_z[rs, 0:depth]
            )
            finish(r, rs, center, sq[y, rs, :] * (lap - adv))

    def acc_rows(t, y, r):
        return acc.at[t, pl.ds(pl.multiple_of(y * span + r, CHUNK), CHUNK), :]

    pressures = (p0, p1, p2)
    for t in range(NT):
        cur = pressures[t]
        vsum[...] = jnp.zeros_like(vsum)

        def forward(y, t=t, cur=cur):
            amount = jnp.where(y.astype(F32) == source_y, wavelet[0, t], 0.0)
            pieces = []

            def finish(r, rs, center, lu):
                value = lu + amount * hot[rs, :]
                acc_rows(t, y, r)[...] = value
                old = p1[y + H, rs, :] if t == 0 else pressures[t - 1][y + H, rs, :]
                new = 2.0 * center - old + value
                if t < NT - 1:
                    pressures[t + 1][y + H, rs, :] = new
                if r < half:
                    pieces.append(new)

            spatial(cur, y, t == 0, finish)
            read = dot(xt[y], jnp.concatenate(split(jnp.concatenate(pieces, axis=0)), axis=1))
            vsum[...] += read[:, 0:depth] + read[:, depth:]

        planes(0, (1, 3, 4)[t], forward)
        if t < NT - 1:
            send(3 + t)
        here = lax.broadcasted_iota(jnp.int32, (nrec, depth), 1).astype(F32) == recz[...]
        residual = jnp.where(here, vsum[...] - obs[t], 0.0)
        hi, lo = split(residual)
        inj[t, :, 0:depth] = hi
        inj[t, :, depth:] = lo

    parts = ((H, rows - 2 * H), (0, H), (rows - H, H))

    def image_copy(d, part, target, source):
        if part < len(parts):
            start, size = parts[part]
            src = outb.at[pl.ds(start, size), target]
            dst = out.at[source, pl.ds(start, size)]
        else:
            src, dst = tailb.at[target], tails.at[source]
        return pltpu.make_async_remote_copy(
            src_ref=src, dst_ref=dst,
            send_sem=image_send.at[d, part], recv_sem=image_recv.at[d, part],
            device_id={"gx": target}, device_id_type=pl.DeviceIdType.MESH)

    def deliver(part):
        for d in range(1, lanes_gx):
            image_copy(d, part, lax.rem(gx + d, lanes_gx), gx).start()

    def delivered(part):
        for d in range(1, lanes_gx):
            image_copy(d, part, lax.rem(gx + d, lanes_gx), gx).wait_send()
            came = lax.rem(gx + lanes_gx - d, lanes_gx)
            image_copy(d, part, came, came).wait_recv()

    adjoint = {3: q3, 2: q2, 1: q1}
    for t in reversed(range(NT)):
        cur = adjoint[t + 1]

        def backward(y, t=t, cur=cur):
            added = dot(xo[y], inj[t])
            added = added[:, 0:depth] + added[:, depth:]
            images = []
            left = []

            def finish(r, rs, center, lu):
                old = q2[y + H, rs, :] if t == NT - 1 else adjoint[t + 2][y + H, rs, :]
                new = 2.0 * center - old + lu
                if r < half:
                    new = new + added[rs]
                if t > 0:
                    adjoint[t][y + H, rs, :] = new
                term = new * acc_rows(t, y, r)[...]
                if t < NT - 1:
                    term = term + acc_rows(t + 1, y, r)[...]
                if t > 0:
                    acc_rows(t, y, r)[...] = term
                else:
                    for k in range(0, CHUNK, 8):
                        value = term[k : k + 8]
                        if left:
                            value = value + left.pop()
                        kept = value.astype(BF).astype(F32)
                        left.append(value - kept)
                        images.append(kept)

            spatial(cur, y, t == NT - 1, finish)
            if t == 0:
                turned = jnp.concatenate(images, axis=0).T
                for g in range(lanes_gx):
                    outb[y, g] = turned[g * layers : (g + 1) * layers].astype(BF)
                carry[y] = left[0]

        planes(0, (6, 5, 2)[t], backward, None if t > 0 else functools.partial(deliver, 0))
        if t > 0:
            send(5 + NT - 1 - t)

    deliver(1)
    deliver(2)
    turned = carry[...].reshape(rows * 8, depth).T
    for g in range(lanes_gx):
        tailb[g] = turned[g * layers : (g + 1) * layers].astype(BF)
    deliver(3)
    own = pltpu.make_async_copy(outb.at[:, gx], out.at[gx], own_sem)
    own_end = pltpu.make_async_copy(tailb.at[gx], tails.at[gx], own_tail)
    own.start()
    own_end.start()
    for r in range(lanes_gx - 1):
        passed(0, r)
        passed(1, r)
    for e in range(7):
        @pl.when(has_left)
        def _():
            to_left(e).wait_send()

        @pl.when(has_right)
        def _():
            to_right(e).wait_send()

    own.wait()
    own_end.wait()
    for part in range(len(parts) + 1):
        delivered(part)


def smooth_kernel(dims, footprint, images, tails, out, field, dist):
    shots, rows, layers, span, cells = dims
    place = lax.axis_index("gx")
    for s in range(shots):
        window = images[s].astype(F32).reshape(rows * layers, span)
        tail = tails[s].astype(F32)
        width = tail.shape[1]
        at_end = lax.broadcasted_iota(jnp.int32, tail.shape, 1) >= width - 8
        ends = [
            jnp.where(at_end, pltpu.roll(tail, width - 8 - 8 * y, 1) if y < rows - 1 else tail, 0.0)
            for y in range(rows)
        ]
        window = jnp.concatenate(
            [window[:, : span - width], window[:, span - width :] + jnp.concatenate(ends, axis=0)], axis=1
        )
        if cells > span:
            window = jnp.concatenate([window, jnp.zeros((rows * layers, cells - span), F32)], axis=1)
        window = pltpu.roll(window, footprint[s, 0] * CX, 1)
        for c in range(cells // 128):
            piece = window[:, c * 128 : (c + 1) * 128]
            if s == 0:
                field[c] = piece
            else:
                field[c] += piece
    dist[...] = jnp.abs(
        lax.broadcasted_iota(jnp.int32, (cells, cells), 0) - lax.broadcasted_iota(jnp.int32, (cells, cells), 1)
    ).astype(F32)

    @pl.loop(0, layers)
    def _(z):
        depth_value = (place * layers + z).astype(F32)
        length = CX * (1.5 + 4.5 * depth_value / (NZ - 1.0))
        rate = -1.0 / jnp.full((8, 128), length, F32)
        rate = rate[0:1, 0:1]
        weights = jnp.exp(dist[...] * rate)
        norm = jnp.sum(weights, axis=0, keepdims=True)
        w_hi, w_lo = split(weights)
        layer = jnp.concatenate(
            [field[c, pl.ds(z, rows, stride=layers), :] for c in range(cells // 128)], axis=1
        )
        f_hi, f_lo = split(layer)
        main = dot(jnp.concatenate([f_hi, f_lo], axis=0), w_hi)
        total = main[0:rows] + main[rows:] + dot(f_hi, w_lo)
        out[z] = total / norm


def on_device(
    velocity, log_density, fwd_prev, fwd_now, adj_now, adj_next,
    wavelet, source_pos, receiver_pos, observed, footprint, owner,
):
    block_count = lax.axis_size("gx")
    block_cells, rows, depth = velocity.shape[1:]
    shots, slots = footprint.shape
    span = slots * block_cells
    half = span // 2
    layers = depth // block_count
    nrec = receiver_pos.shape[2]
    first_x, second_x = band(span)
    first_z, second_z = band(depth)
    dx = jnp.asarray(np.concatenate([first_x, second_x], 0), BF)
    one = np.concatenate([first_z.T, second_z.T], 1)
    mz = jnp.asarray(np.concatenate([one, one], 0), BF)
    flat = lambda a: a.reshape(a.shape[1] * rows, depth)
    vm = pl.BlockSpec(memory_space=pltpu.VMEM)
    sm = pl.BlockSpec(memory_space=pltpu.SMEM)
    padded = pltpu.VMEM((rows + 2 * H, span, depth), F32)
    received, tails = pl.pallas_call(
        functools.partial(wave_kernel, (rows, span, depth, block_cells)),
        out_shape=(
            jax.ShapeDtypeStruct((block_count, rows, layers, span), BF),
            jax.ShapeDtypeStruct((block_count, layers, rows * 8), BF),
        ),
        in_specs=[sm] * 4 + [vm] * 10,
        out_specs=(pl.BlockSpec(memory_space=pl.ANY),) * 2,
        scratch_shapes=[
            padded, padded, padded, padded, padded, padded,
            pltpu.VMEM((NT, rows * span, depth), F32),
            pltpu.VMEM((rows, span, depth), F32),
            pltpu.VMEM((3, rows, span, depth), F32),
            pltpu.VMEM((rows + 2 * H, span, depth), BF),
            pltpu.VMEM((rows, nrec, half), BF),
            pltpu.VMEM((rows, half, nrec), BF),
            pltpu.VMEM((span, depth), F32),
            pltpu.VMEM((nrec, depth), F32),
            pltpu.VMEM((NT, nrec, 2 * depth), BF),
            pltpu.VMEM((block_count, block_cells * rows, depth), BF),
            pltpu.VMEM((block_count, block_cells * rows, depth), BF),
            pltpu.VMEM((span, depth), F32),
            pltpu.VMEM((NT, nrec, depth), F32),
            pltpu.VMEM((nrec, depth), F32),
            pltpu.VMEM((rows, block_count, layers, span), BF),
            pltpu.VMEM((rows, 8, depth), F32),
            pltpu.VMEM((block_count, layers, rows * 8), BF),
            pltpu.SemaphoreType.DMA((7, 2)),
            pltpu.SemaphoreType.DMA((7, 2)),
            pltpu.SemaphoreType.DMA((2, 2, block_count)),
            pltpu.SemaphoreType.DMA((2, 2, block_count)),
            pltpu.SemaphoreType.DMA((block_count, 4)),
            pltpu.SemaphoreType.DMA((block_count, 4)),
            pltpu.SemaphoreType.DMA,
            pltpu.SemaphoreType.DMA,
        ],
        compiler_params=pltpu.CompilerParams(
            collective_id=0, has_side_effects=True, vmem_limit_bytes=60 * 1024 * 1024
        ),
        name="wave",
    )(
        source_pos, wavelet, footprint, owner,
        flat(fwd_prev), flat(fwd_now), flat(adj_now), flat(adj_next), flat(velocity), flat(log_density),
        receiver_pos[0], observed[0], dx, mz,
    )
    cells = block_count * block_cells
    return pl.pallas_call(
        functools.partial(smooth_kernel, (shots, rows, layers, span, cells)),
        out_shape=jax.ShapeDtypeStruct((layers, rows, cells), F32),
        in_specs=[sm, vm, vm],
        out_specs=vm,
        scratch_shapes=[
            pltpu.VMEM((cells // 128, rows * layers, 128), F32),
            pltpu.VMEM((cells, cells), F32),
        ],
        compiler_params=pltpu.CompilerParams(vmem_limit_bytes=56 * 1024 * 1024),
        name="smooth",
    )(footprint, received, tails)


def solution(mesh):
    shared = P(("grp", "gx"), None, "gy", None)
    placed = (shared,) * 6 + (
        P(("grp", "gx"), None),
        P(("grp", "gx"), None),
        P(("grp", "gx"), None, None),
        P(("grp", "gx"), None, None),
        P("grp", None),
        P(),
    )
    return jax.shard_map(
        on_device,
        mesh=mesh,
        in_specs=placed,
        out_specs=P(("grp", "gx"), "gy", None),
        check_vma=False,
    )
```
